32 devices in a mesh: outer: 4 (over z), inner: 2 (over x), head: 4 (over y, core).
Axes of the slice: x: 2, y: 2, z: 4, core: 2. Of those that a mesh axis runs over, the one named last changes fastest.
Arguments:
- queries: bfloat16 [1536, 20, 128], P(('outer', 'inner', 'head')), may hold values from -400 to 400
- keys: bfloat16 [1536, 20, 128], P(('outer', 'inner', 'head')), may hold values from -12 to 12
- values: bfloat16 [1536, 20, 128], P(('outer', 'inner', 'head')), may hold values from -6 to 6
- tan_queries: bfloat16 [1536, 20, 128], P(('outer', 'inner', 'head')), may hold values from -6 to 6
- tan_keys: bfloat16 [1536, 20, 128], P(('outer', 'inner', 'head')), may hold values from -6 to 6
- tan_values: bfloat16 [1536, 20, 128], P(('outer', 'inner', 'head')), may hold values from -6 to 6
Outputs:
- out: bfloat16 [1536, 20, 128], P(('outer', 'inner'), 'head')
- lse: float32 [20, 1536], P('head', ('outer', 'inner'))
- tan_out: bfloat16 [1536, 20, 128], P(('outer', 'inner'), 'head')
- tan_lse: float32 [20, 1536], P('head', ('outer', 'inner'))
The draws below stay inside these ranges and needn't reach their ends.
All inputs are finite; a program needn't handle non-finite values.
Results may differ from the reference program's by a relative error of at most 0.012.
Values may be sent and summed in bfloat16 or wider, within the bound.
No kernel may reach another device: no remote copies, remote signals or barrier semaphores. Data moves between devices by JAX's collectives and lax.ppermute only.
A program may use at most 64 MiB of HBM per device.

```python
import jax
import jax.numpy as jnp
from jax import lax

HD = 128
HEADS = 20
QROWS = 192
TOKENS = 1536
N_OUTER = 4
N_INNER = 2


def shared_keys(key):
    position = jnp.arange(TOKENS, dtype=jnp.int32)[:, None, None]
    drawn_keys = jnp.clip(jax.random.normal(jax.random.fold_in(key, 101), (TOKENS, HEADS, HD), jnp.float32), -6.0, 6.0)
    blended = drawn_keys
    return jnp.where(position % 8 == 4, blended, drawn_keys)


def draw_keys(key, part):
    return shared_keys(key).astype(jnp.bfloat16)


def draw_queries(key, part):
    key = jax.random.fold_in(key, 7)
    return (2.0 * jnp.clip(jax.random.normal(key, (TOKENS, HEADS, HD), jnp.float32), -6.0, 6.0)).astype(jnp.bfloat16)


def levels(stream_key, dims, cuts, smallest, top_value):
    loudness, own = 1.0, jax.random.fold_in(stream_key, 6)
    for dim, blocks in cuts:
        heights = jnp.exp(jax.random.uniform(jax.random.fold_in(own, dim), (blocks,), jnp.float32, smallest / len(cuts), top_value / len(cuts)))
        loudness = loudness * jnp.repeat(heights, dims[dim] // blocks).reshape([-1 if axis == dim else 1 for axis in range(len(dims))])
    return loudness


def noise(stream_key, extent, scale, reach, pieces=(), held_as=jnp.bfloat16):
    factor_of = levels(stream_key, extent, pieces, -0.22, 0.18) if pieces else 1.0
    drawn = jax.random.normal(stream_key, extent, jnp.float32) * scale * factor_of
    return jnp.minimum(jnp.maximum(drawn, -reach), reach).astype(held_as)


def setup_inputs(seed: int = 0) -> dict:
    streams_of = jax.random.split(jax.random.key(seed), 7)
    return {
        "queries": draw_queries(jax.random.fold_in(streams_of[6], 71), 0),
        "keys": draw_keys(jax.random.fold_in(streams_of[6], 71), 0),
        "values": noise(streams_of[2], (TOKENS, HEADS, HD), 1.0, 6.0, ((0, 32),)),
        "tan_queries": noise(streams_of[3], (TOKENS, HEADS, HD), 1.0, 6.0, ((0, 32),)),
        "tan_keys": noise(streams_of[4], (TOKENS, HEADS, HD), 1.0, 6.0, ((0, 32),)),
        "tan_values": noise(streams_of[5], (TOKENS, HEADS, HD), 1.0, 6.0, ((0, 32),)),
    }


def reference(queries, keys, values, tan_queries, tan_keys, tan_values):
    shards = N_OUTER * N_INNER

    def by_shard(array):
        return array.reshape(N_OUTER, N_INNER, QROWS, HEADS, HD)

    key_grid = by_shard(keys)
    value_grid = by_shard(values)
    tan_key_grid = by_shard(tan_keys)
    tan_value_grid = by_shard(tan_values)
    query_rows = queries.reshape(shards, QROWS, HEADS, HD)
    tan_query_rows = tan_queries.reshape(shards, QROWS, HEADS, HD)
    score_scale = HD ** -0.5

    def window_state(shard_index):
        outer_pos = shard_index // N_INNER
        inner_pos = shard_index % N_INNER
        picks = []
        for outer_back in range(2):
            for inner_back in range(3):
                picks.append(((outer_pos - outer_back) % N_OUTER, (inner_pos - inner_back) % N_INNER))

        def window(grid):
            return jnp.concatenate([grid[outer_row, inner_col] for outer_row, inner_col in picks], axis=0).astype(jnp.float32)

        win_keys = window(key_grid)
        win_values = window(value_grid)
        win_tan_keys = window(tan_key_grid)
        win_tan_values = window(tan_value_grid)
        own_queries = query_rows[shard_index].astype(jnp.float32)
        own_tangents = tan_query_rows[shard_index].astype(jnp.float32)
        scores = jnp.einsum("qhd,khd->hqk", own_queries, win_keys) * score_scale
        tan_scores = (jnp.einsum("qhd,khd->hqk", own_tangents, win_keys) + jnp.einsum("qhd,khd->hqk", own_queries, win_tan_keys)) * score_scale
        highest = jnp.max(scores, axis=2)
        weights = jnp.exp(scores - highest[:, :, None])
        totals = jnp.sum(weights, axis=2)
        tilted = weights * tan_scores
        slopes = jnp.sum(tilted, axis=2)
        probs = lax.optimization_barrier(weights.astype(jnp.bfloat16)).astype(jnp.float32)
        tilted_round = lax.optimization_barrier(tilted.astype(jnp.bfloat16)).astype(jnp.float32)
        out_full = jnp.einsum("hqk,khd->qhd", probs, win_values) / totals.T[:, :, None]
        tan_lse = slopes / totals
        lse = highest + jnp.log(totals)
        tan_sum = jnp.einsum("hqk,khd->qhd", tilted_round, win_values) + jnp.einsum("hqk,khd->qhd", probs, win_tan_values)
        tan_out = tan_sum / totals.T[:, :, None] - tan_lse.T[:, :, None] * out_full
        return out_full.astype(jnp.bfloat16), lse, tan_out.astype(jnp.bfloat16), tan_lse

    out, lse, tan_out, tan_lse = lax.map(window_state, jnp.arange(shards, dtype=jnp.int32))
    out = out.reshape(TOKENS, HEADS, HD)
    tan_out = tan_out.reshape(TOKENS, HEADS, HD)
    lse = jnp.transpose(lse, (1, 0, 2)).reshape(HEADS, TOKENS)
    tan_lse = jnp.transpose(tan_lse, (1, 0, 2)).reshape(HEADS, TOKENS)
    return (out, lse, tan_out, tan_lse)
```

```python
import functools
import math

import jax
import jax.numpy as jnp
from jax import lax
from jax.experimental import pallas as pl
from jax.experimental.pallas import tpu as pltpu
from jax.sharding import PartitionSpec as P

VMEM = pltpu.VMEM


def shifted(value, axis, steps):
    count = lax.axis_size(axis)
    pairs = [(source, (source + steps) % count) for source in range(count)]
    return lax.ppermute(value, axis, pairs)


def inner_reach(bundle_part):
    nearby = shifted(bundle_part, "inner", 1)
    farther = shifted(nearby, "inner", 1)
    return (nearby, farther)


def outer_step(bundle_part):
    return shifted(bundle_part, "outer", 1)


def absorb(carried, key_block, own_queries, own_tangents):
    highest, totals, slopes, acc_out, acc_tan = carried
    score_scale = own_queries.shape[-1] ** (-0.5)
    scores = (
        jnp.einsum("qhd,khd->hqk", own_queries, key_block[0], preferred_element_type=jnp.float32)
        * score_scale
    )
    tan_scores = (
        jnp.einsum("qhd,khd->hqk", own_tangents, key_block[0], preferred_element_type=jnp.float32)
        + jnp.einsum("qhd,khd->hqk", own_queries, key_block[2], preferred_element_type=jnp.float32)
    ) * score_scale
    new_highest = jnp.maximum(highest, jnp.max(scores, axis=2))
    weights = jnp.exp(scores - new_highest[:, :, None])
    damping = jnp.exp(highest - new_highest)
    tilted = weights * tan_scores
    totals = totals * damping + jnp.sum(weights, axis=2)
    slopes = slopes * damping + jnp.sum(tilted, axis=2)
    probs = weights.astype(jnp.bfloat16)
    tilted_round = tilted.astype(jnp.bfloat16)
    row_damping = damping.T[:, :, None]
    acc_out = acc_out * row_damping + jnp.einsum(
        "hqk,khd->qhd", probs, key_block[1], preferred_element_type=jnp.float32
    )
    acc_tan = (
        acc_tan * row_damping
        + jnp.einsum("hqk,khd->qhd", tilted_round, key_block[1], preferred_element_type=jnp.float32)
        + jnp.einsum("hqk,khd->qhd", probs, key_block[3], preferred_element_type=jnp.float32)
    )
    return (new_highest, totals, slopes, acc_out, acc_tan)


def on_device_any(queries, keys, values, tan_queries, tan_keys, tan_values):
    packed = jnp.stack((queries, tan_queries, keys, values, tan_keys, tan_values))
    spread = lax.all_to_all(packed, "head", split_axis=2, concat_axis=1, tiled=True)
    own_queries = spread[0]
    own_tangents = spread[1]
    bundle = spread[2:]
    row_count = bundle.shape[1]
    head_count = bundle.shape[2]
    depth = bundle.shape[3]
    behind = outer_step(bundle)
    paired = jnp.concatenate((bundle, behind), axis=1)
    nearby, farther = inner_reach(paired)
    stacks = (paired, nearby, farther)
    carried = (
        jnp.full((head_count, row_count), -jnp.inf, jnp.float32),
        jnp.zeros((head_count, row_count), jnp.float32),
        jnp.zeros((head_count, row_count), jnp.float32),
        jnp.zeros((row_count, head_count, depth), jnp.float32),
        jnp.zeros((row_count, head_count, depth), jnp.float32),
    )
    for whole_stack in stacks:
        for offset in range(0, whole_stack.shape[1], row_count):
            carried = absorb(
                carried, whole_stack[:, offset : offset + row_count], own_queries, own_tangents
            )
    highest, totals, slopes, acc_out, acc_tan = carried
    row_totals = totals.T[:, :, None]
    out_full = acc_out / row_totals
    lse = highest + jnp.log(totals)
    tan_lse = slopes / totals
    tan_out = acc_tan / row_totals - tan_lse.T[:, :, None] * out_full
    return (out_full.astype(jnp.bfloat16), lse, tan_out.astype(jnp.bfloat16), tan_lse)


PLACES_A = ((0, 0), (0, 1), (1, 0), (1, 1), (0, 2), (0, 3), (1, 2), (1, 3))


def move(value, inner_flip, head_flip, heads_axis):
    if inner_flip == 0:
        pairs = [(h, h ^ head_flip) for h in range(heads_axis)]
        return lax.ppermute(value, "head", pairs)
    pairs = [
        (i * heads_axis + h, (i ^ inner_flip) * heads_axis + (h ^ head_flip))
        for i in range(2)
        for h in range(heads_axis)
    ]
    return lax.ppermute(value, ("inner", "head"), pairs)


def move_up(value, outer_count, heads_axis, head_flip=0):
    if head_flip == 0:
        return lax.ppermute(value, "outer", [(o, (o + 1) % outer_count) for o in range(outer_count)])
    pairs = [
        (o * heads_axis + h, ((o + 1) % outer_count) * heads_axis + (h ^ head_flip))
        for o in range(outer_count)
        for h in range(heads_axis)
    ]
    return lax.ppermute(value, ("outer", "head"), pairs)


def after(value, *earlier):
    return lax.optimization_barrier((value,) + earlier)[0]


def kernel_call(body, ins, outs, scratch=(), flops=0, moved=0, vmem=16 << 20):
    return pl.pallas_call(
        body,
        out_shape=outs,
        in_specs=[pl.BlockSpec(memory_space=VMEM)] * ins,
        out_specs=[pl.BlockSpec(memory_space=VMEM)] * len(outs),
        scratch_shapes=scratch,
        compiler_params=pltpu.CompilerParams(vmem_limit_bytes=vmem),
        cost_estimate=pl.CostEstimate(flops=flops, bytes_accessed=moved, transcendentals=0),
    )


def pack_first(hg, na, *refs):
    arrays, outs = refs[:4], refs[4:]
    h, x = lax.axis_index("head"), lax.axis_index("inner")
    for out, (mx, m) in zip(outs, PLACES_A):
        base = hg * (h ^ m) + na * (x ^ mx)
        for a, array in enumerate(arrays):
            out[a * na : (a + 1) * na] = array[pl.ds(base, na)]


def pack_second(hg, na, *refs):
    keys_side, query_side, outs = refs[:4], refs[4:6], refs[6:]
    h, x = lax.axis_index("head"), lax.axis_index("inner")
    for out, (mx, m) in zip(outs, PLACES_A):
        group = hg * (h ^ m)
        base = group + na * (x ^ mx)
        for a, array in enumerate(keys_side):
            out[a] = array[group + hg - 1]
        for a, array in enumerate(query_side):
            out[4 + a * na : 4 + (a + 1) * na] = array[pl.ds(base, na)]
        if mx == 0:
            for a, array in enumerate(query_side):
                out[4 + 2 * na + a] = array[group + hg - 1]
        if (mx, m) == (0, 1):
            for a, array in enumerate(keys_side):
                at = 6 + 2 * na + a * na
                out[at : at + na] = array[pl.ds(base, na)]


def fill(dst, row, rows, first, second):
    depth = first.shape[-1]
    dst[pl.ds(row, rows), 0:depth] = first
    dst[pl.ds(row, rows), depth : 2 * depth] = second


def attend(qq, kk, vv, own, far):
    depth = qq.shape[-1] // 2
    half = kk.shape[0] // 2
    scale = depth ** (-0.5)
    across = (((1,), (1,)), ((), ()))
    along = (((1,), (0,)), ((), ()))
    dot = functools.partial(lax.dot_general, preferred_element_type=jnp.float32)
    scores = dot(qq[:, depth:], kk[:, 0:depth], across)
    tan_scores = dot(qq[...], kk[...], across)
    highest = jnp.max(scores, axis=1, keepdims=True)
    weights = jnp.exp2((scores - highest) * (scale * math.log2(math.e)))
    tilted = weights * (tan_scores * scale)

    def both(value):
        left = jnp.sum(value[:, :half], axis=1, keepdims=True)
        right = jnp.sum(value[:, half:], axis=1, keepdims=True)
        return own * left + far * right

    totals, slopes = both(weights), both(tilted)
    probs = weights.astype(jnp.bfloat16)
    tilted_round = tilted.astype(jnp.bfloat16)
    acc = own * dot(probs[:, :half], vv[0:half, :], along) + far * dot(
        probs[:, half:], vv[half:, :], along
    )
    acc_tan = own * dot(tilted_round[:, :half], vv[0:half, 0:depth], along) + far * dot(
        tilted_round[:, half:], vv[half:, 0:depth], along
    )
    share = 1.0 / totals
    out_full = acc[:, 0:depth] * share
    tan_lse = slopes * share
    tan_out = (acc[:, depth:] + acc_tan) * share - tan_lse * out_full
    lse = highest * scale + jnp.log(totals)
    return out_full, tan_out, lse, tan_lse


def columns_to_rows(columns, rows):
    lane = lax.broadcasted_iota(jnp.int32, (columns[0].shape[0], 128), 1)
    wide = jnp.zeros(lane.shape, jnp.float32)
    for i, column in enumerate(columns):
        wide = jnp.where(lane == i, column, wide)
    return wide.T[0:rows]


def attend_a(na, layout, *refs):
    count = layout["refs"]
    ins = refs[:count]
    mine, mine_rows, send, send_rows = refs[count : count + 4]
    kks, vvs, qqs = refs[count + 4 :]
    h = lax.axis_index("head")
    tokens = ins[0].shape[1]
    span = qqs.shape[1] // 2
    columns = ([], [])
    for j in range(na):
        kk, vv, qq = kks.at[j], vvs.at[j], qqs.at[j]
        for r, (i, at) in enumerate(layout["keys"]):
            k, v, tk, tv = (ins[i][at + a * na + j] for a in range(4))
            fill(kk, r * tokens, tokens, k, tk)
            fill(vv, r * tokens, tokens, v, tv)
        for mx in range(2):
            for m, (i, at) in enumerate(layout["queries"][mx]):
                row = pl.multiple_of(mx * span + (h ^ m) * tokens, 16)
                fill(qq, row, tokens, ins[i][at + na + j], ins[i][at + j])
        for mx in range(2):
            own, far = (2.0, 1.0) if mx == 0 else (1.0, 2.0)
            out, tan_out, lse, tan_lse = attend(qq.at[mx * span : (mx + 1) * span], kk, vv, own, far)
            to = (mine, send)[mx]
            to[j] = out.astype(jnp.bfloat16)
            to[na + j] = tan_out.astype(jnp.bfloat16)
            columns[mx].extend((lse, tan_lse))
    mine_rows[...] = columns_to_rows(columns[0], 8)
    send_rows[...] = columns_to_rows(columns[1], 8)


def attend_b(na, layout, *refs):
    count = layout["refs"]
    ins = refs[:count]
    mine, mine_rows, got, got_rows = refs[count : count + 4]
    out_ref, lse_ref, tan_ref, tan_lse_ref = refs[count + 4 : count + 8]
    kk, vv, qq = refs[count + 8 :]
    h, x = lax.axis_index("head"), lax.axis_index("inner")
    tokens = ins[0].shape[1]
    for r, (i, at) in enumerate(layout["keys"]):
        k, v, tk, tv = (ins[i][at + a] for a in range(4))
        fill(kk, r * tokens, tokens, k, tk)
        fill(vv, r * tokens, tokens, v, tv)
    for m, (i, at) in enumerate(layout["queries"]):
        row = pl.multiple_of((h ^ m) * tokens, 16)
        fill(qq, row, tokens, ins[i][at + 1], ins[i][at])
    out, tan_out, lse, tan_lse = attend(qq, kk, vv, 2.0, 1.0)
    out_ref[2 * na] = out.astype(jnp.bfloat16)
    tan_ref[2 * na] = tan_out.astype(jnp.bfloat16)
    rows = columns_to_rows([lse, tan_lse], 8)
    lse_ref[2 * na : 2 * na + 1] = rows[0:1]
    tan_lse_ref[2 * na : 2 * na + 1] = rows[1:2]
    for source, source_rows, place in ((mine, mine_rows, x), (got, got_rows, 1 - x)):
        for j in range(na):
            head = place * na + j
            out_ref[head] = source[j]
            tan_ref[head] = source[na + j]
            lse_ref[pl.ds(head, 1)] = source_rows[2 * j : 2 * j + 1]
            tan_lse_ref[pl.ds(head, 1)] = source_rows[2 * j + 1 : 2 * j + 2]


def on_device_pair(queries, keys, values, tan_queries, tan_keys, tan_values):
    outer_count, heads_axis = lax.axis_size("outer"), lax.axis_size("head")
    tokens, heads, depth = keys.shape
    hg = heads // heads_axis
    na = hg // 2
    span = tokens * heads_axis
    bf16, f32 = jnp.bfloat16, jnp.float32
    move_to = functools.partial(move, heads_axis=heads_axis)
    up = functools.partial(move_up, outer_count=outer_count, heads_axis=heads_axis)
    cat = lambda *parts: jnp.concatenate(parts, axis=0)
    units = lambda n: jax.ShapeDtypeStruct((n, tokens, depth), bf16)

    q, k, v, tq, tk, tv = (
        a.transpose(1, 0, 2) for a in (queries, keys, values, tan_queries, tan_keys, tan_values)
    )
    unit_bytes = tokens * depth * 2
    ka = 4 * na
    a_own, a_c, xa0, xa1, ya0, ya1, xya0, xya1 = kernel_call(
        functools.partial(pack_first, hg, na),
        4,
        [units(ka)] * 8,
        moved=8 * ka * 2 * unit_bytes,
    )(k, v, tk, tv)
    with_q, with_both = 4 + 2 * na, 6 + 2 * na
    sizes = [with_both if mx == 0 else with_q for mx, m in PLACES_A]
    sizes[1] += ka
    b_own, b_c, xb0, xb1, yb0, yb1, xyb0, xyb1 = kernel_call(
        functools.partial(pack_second, hg, na),
        6,
        [units(n) for n in sizes],
        moved=sum(sizes) * 2 * unit_bytes,
    )(k, v, tk, tv, q, tq)

    xa0, xa1 = move_to(xa0, 1, 0), move_to(xa1, 1, 1)
    za0, za1 = up(a_own), up(a_c, head_flip=1)
    ya0, ya1 = move_to(ya0, 0, 2), move_to(ya1, 0, 3)
    xya0, xya1 = move_to(after(xya0, xa0), 1, 2), move_to(after(xya1, xa1), 1, 3)
    cc = move_to(b_c, 0, 1)
    zx = up(after(cat(xa0, xa1), za0))
    zy = up(after(cat(ya0, ya1), za1))
    zxy = up(after(cat(xya0, xya1), zx))
    xb0, xb1 = move_to(after(xb0, xya0), 1, 0), move_to(after(xb1, xya1), 1, 1)
    yb0, yb1 = move_to(after(yb0, ya1), 0, 2), move_to(after(yb1, ya1), 0, 3)
    xyb0, xyb1 = move_to(after(xyb0, xb0), 1, 2), move_to(after(xyb1, xb1), 1, 3)
    zb0 = up(after(cat(b_own[:4], cc[:4], yb0[:4], yb1[:4]), zy))
    zb1 = up(after(cat(xb0[:4], xb1[:4], xyb0[:4], xyb1[:4]), zxy))

    scratch = lambda q_rows: [
        VMEM((4 * span, 2 * depth), bf16),
        VMEM((4 * span, 2 * depth), bf16),
        VMEM((q_rows, 2 * depth), bf16),
    ]
    work = span * 4 * span * depth * 12
    a_ins = [a_own, cc, ya0, ya1, za0, za1, zy, xa0, xa1, xya0, xya1, zx, zxy, b_own, yb0, yb1, xb0, xb1, xyb0, xyb1]
    a_layout = {
        "refs": len(a_ins),
        "keys": [(0, 0), (1, with_both), (2, 0), (3, 0), (4, 0), (5, 0), (6, 0), (6, ka)]
        + [(7, 0), (8, 0), (9, 0), (10, 0), (11, 0), (11, ka), (12, 0), (12, ka)],
        "queries": [[(13, 4), (1, 4), (14, 4), (15, 4)], [(16, 4), (17, 4), (18, 4), (19, 4)]],
    }
    results = jax.ShapeDtypeStruct((2 * na, span, depth), bf16)
    rows = jax.ShapeDtypeStruct((8, span), f32)
    mine, mine_rows, send, send_rows = kernel_call(
        functools.partial(attend_a, na, a_layout),
        len(a_ins),
        [results, rows, results, rows],
        [VMEM((na,) + s.shape, bf16) for s in scratch(2 * span)],
        flops=work * 2 * na,
        moved=1 << 20,
    )(*a_ins)
    got, got_rows = move_to(send, 1, 0), move_to(send_rows, 1, 0)

    b_ins = [b_own, cc, yb0, yb1, zb0, xb0, xb1, xyb0, xyb1, zb1]
    b_layout = {
        "refs": len(b_ins),
        "keys": [(0, 0), (1, 0), (2, 0), (3, 0), (4, 0), (4, 4), (4, 8), (4, 12)]
        + [(5, 0), (6, 0), (7, 0), (8, 0), (9, 0), (9, 4), (9, 8), (9, 12)],
        "queries": [(0, with_q), (1, with_q), (2, with_q), (3, with_q)],
    }
    full = jax.ShapeDtypeStruct((hg, span, depth), bf16)
    full_rows = jax.ShapeDtypeStruct((hg, span), f32)
    out, lse, tan_out, tan_lse = kernel_call(
        functools.partial(attend_b, na, b_layout),
        len(b_ins) + 4,
        [full, full_rows, full, full_rows],
        scratch(span),
        flops=work,
        moved=1 << 20,
    )(*b_ins, mine, mine_rows, got, got_rows)
    return out.transpose(1, 0, 2), lse, tan_out.transpose(1, 0, 2), tan_lse


def solution(mesh):
    def per_device(queries, *others):
        group = queries.shape[1] // mesh.shape["head"]
        paired = mesh.shape["inner"] == 2 and mesh.shape["head"] == 4 and group % 2 == 1
        paired = paired and queries.shape[0] % 16 == 0
        return (on_device_pair if paired else on_device_any)(queries, *others)

    tokens_split = P(("outer", "inner", "head"), None, None)
    return jax.shard_map(
        per_device,
        mesh=mesh,
        in_specs=(tokens_split,) * 6,
        out_specs=(
            P(("outer", "inner"), "head", None),
            P("head", ("outer", "inner")),
            P(("outer", "inner"), "head", None),
            P("head", ("outer", "inner")),
        ),
        check_vma=False,
    )
```
